32 devices in a mesh: groups: 2 (over y), wide: 4 (over z), narrow: 2 (over x), sub: 2 (over core).
Axes of the slice: x: 2, y: 2, z: 4, core: 2. Of those that a mesh axis runs over, the one named last changes fastest.
Arguments:
- tokens: bfloat16 [128, 8192], P(('groups', 'wide', 'sub'), 'narrow'), parts along dimension 0, may hold values from -6 to 6
- gate_weight: bfloat16 [8192, 26624], P('narrow', ('wide', 'sub')), may hold values from -0.0625 to 0.0625
- up_weight: bfloat16 [8192, 26624], P('narrow', ('wide', 'sub')), may hold values from -0.0625 to 0.0625
- down_weight: bfloat16 [26624, 8192], P(('wide', 'sub'), 'narrow'), may hold values from -0.0390625 to 0.0390625
Outputs:
- block_out: bfloat16 [128, 8192], P(('groups', 'wide', 'sub'), 'narrow'), parts along dimension 0
The draws below stay inside these ranges and needn't reach their ends.
There are 2 independent parts, one for each index of `groups`. The reference program is written for one: setup_inputs(seed, part) draws one part's arguments, and reference() takes and returns one part's arrays. A program takes and returns all parts, laid end to end along the dimension named above; an argument that names none is the same for every part. Nothing has to cross between parts.
All inputs are finite; a program needn't handle non-finite values.
Results may differ from the reference program's by a relative error of at most 0.005.
Values may be sent and summed in bfloat16 or wider, within the bound.
A program may use at most 192 MiB of HBM per device.

```python
import jax
import jax.numpy as jnp

D = 8192
FF = 26624
TOKENS = 64


def block_levels(key, extent, split, low, largest):
    factor_of = 1.0
    for position, shards_of in split:
        steps = jax.random.uniform(jax.random.fold_in(jax.random.fold_in(key, 6), position), (shards_of,), jnp.float32, low / len(split), largest / len(split))
        factor_of = factor_of * jnp.repeat(jnp.exp(steps), extent[position] // shards_of).reshape((-1,) + (1,) * (len(extent) - 1 - position))
    return factor_of


def gaussian(stream_key, extent, scale, most, shards=(), dtype=jnp.bfloat16):
    drawn = jax.random.normal(stream_key, extent, jnp.float32) * scale
    if len(shards) > 0:
        drawn = block_levels(stream_key, extent, shards, -0.22, 0.18) * drawn
    return jnp.clip(drawn, min=-most, max=most).astype(dtype)


def setup_inputs(seed: int = 0, part: int = 0) -> dict:
    splits = jax.random.split(jax.random.key(seed), 5)
    part_keys = jax.random.split(jax.random.fold_in(splits[4], part), 5)
    tokens = gaussian(part_keys[0], (TOKENS, D), 1.0, 6.0, ((0, 8), (1, 2)))
    gate_weight = gaussian(splits[1], (D, FF), D ** -0.5, 0.0625, ((0, 2), (1, 8)))
    up_weight = gaussian(splits[2], (D, FF), D ** -0.5, 0.0625, ((0, 2), (1, 8)))
    down_weight = gaussian(splits[3], (FF, D), FF ** -0.5, 0.0390625, ((0, 8), (1, 2)))
    return dict(tokens=tokens, gate_weight=gate_weight, up_weight=up_weight, down_weight=down_weight)


def reference(tokens, gate_weight, up_weight, down_weight):
    gate = jnp.dot(tokens, gate_weight, preferred_element_type=jnp.float32)
    up = jnp.dot(tokens, up_weight, preferred_element_type=jnp.float32)
    hidden = (jax.nn.silu(gate) * up).astype(jnp.bfloat16)
    return jnp.dot(hidden, down_weight, preferred_element_type=jnp.float32).astype(jnp.bfloat16)
```

```python
import functools

import jax
import jax.numpy as jnp
from jax import lax
from jax.experimental import pallas as pl
from jax.experimental.pallas import tpu as pltpu
from jax.sharding import PartitionSpec as P

MESH = pl.DeviceIdType.MESH
F32 = jnp.float32
BF16 = jnp.bfloat16


def plain(tokens, gate_weight, up_weight, down_weight):
    segment = lax.all_gather(tokens, ("wide", "sub"), axis=0, tiled=True)
    gate_part = jnp.dot(segment, gate_weight, preferred_element_type=F32)
    up_part = jnp.dot(segment, up_weight, preferred_element_type=F32)
    totals = lax.psum(jnp.stack([gate_part, up_part]), "narrow")
    hidden = (jax.nn.silu(totals[0]) * totals[1]).astype(BF16)
    output_block = lax.psum_scatter(
        jnp.dot(hidden, down_weight, preferred_element_type=F32),
        ("wide", "sub"),
        scatter_dimension=0,
        tiled=True,
    )
    return output_block.astype(BF16)


def chunks_of(extent, width):
    return [(o, min(width, extent - o)) for o in range(0, extent, width)]


def kernel(W, chunks, down_groups, tiles,
           x_ref, gate_ref, up_ref, down_ref, out_ref,
           wg, wu, wd, tok, T, own, xsend, xrecv, hid, acc, srecv, ysend, yrecv, oacc, zsend, zrecv,
           wg_sem, wu_sem, wd_sem, tz_s, ty_s, tc_s, t_r, p_s, p_r, h_s, h_r,
           s_s, s_r, y_s, y_r, z_s, z_r):
    g, w, n, s = (lax.axis_index(a) for a in ("groups", "wide", "narrow", "sub"))
    B, D = x_ref.shape
    HU = wg.shape[1]
    R = T.shape[0]
    R2, R4 = R // 2, R // 4

    def weight_copy(src, dst, sems, c, rows):
        o, k = chunks[c]
        at = pl.ds(pl.multiple_of(g * HU + o, 128), k)
        if rows:
            return pltpu.make_async_copy(src.at[at, :], dst.at[pl.ds(o, k), :], sems.at[c])
        return pltpu.make_async_copy(src.at[:, at], dst.at[:, pl.ds(o, k)], sems.at[c])

    gates = [weight_copy(gate_ref, wg, wg_sem, c, False) for c in range(len(chunks))]
    ups = [weight_copy(up_ref, wu, wu_sem, c, False) for c in range(len(chunks))]
    downs = [weight_copy(down_ref, wd, wd_sem, c, True) for c in range(len(chunks))]
    for c in range(len(chunks)):
        gates[c].start()
        ups[c].start()
    for d in downs:
        d.start()

    def remote(src, dst, send, recv, **to):
        return pltpu.make_async_remote_copy(
            src_ref=src, dst_ref=dst, send_sem=send, recv_sem=recv, device_id=to, device_id_type=MESH)

    others = [lax.rem(w + d, W) for d in range(1, W)]
    barrier = pltpu.get_barrier_semaphore()
    for to in [{"wide": o} for o in others] + [{"groups": 1 - g}, {"sub": 1 - s}, {"narrow": 1 - n}]:
        pl.semaphore_signal(barrier, inc=1, device_id=to, device_id_type=MESH)
    x = x_ref[...].astype(F32)
    block = lambda gg, ww, ss: ss * (2 * W) + gg * W + ww
    me = block(g, w, s)
    tok[me] = jnp.concatenate([x[:, : D // 2], x[:, D // 2:]], axis=0).astype(BF16)
    pl.semaphore_wait(barrier, W + 2)

    sends = []

    def go(copy):
        copy.start()
        sends.append(copy)

    def to_z(b, o):
        return remote(tok.at[b], tok.at[b], tz_s.at[o], t_r.at[b], wide=o)

    def to_y(b, o):
        return remote(tok.at[b], tok.at[b], ty_s.at[o], t_r.at[b], groups=1 - g)

    def to_core(b, i):
        return remote(tok.at[b], tok.at[b], tc_s.at[i], t_r.at[b], sub=1 - s)

    for o in others:
        go(to_z(me, o))
    go(to_y(me, w))
    go(to_core(me, g * W + w))
    for o in others:
        b = block(g, o, s)
        to_z(b, o).wait_recv()
        go(to_y(b, o))
        go(to_core(b, g * W + o))
    for o in [w] + others:
        b = block(1 - g, o, s)
        to_y(b, o).wait_recv()
        go(to_core(b, (1 - g) * W + o))
    for gg in range(2):
        for ww in range(W):
            to_core(block(gg, ww, 1 - s), gg * W + ww).wait_recv()

    for j in range(R // 16):
        a = tok[2 * j].astype(F32)
        b = tok[2 * j + 1].astype(F32)
        T[16 * j:16 * j + 16, : D // 2] = jnp.concatenate([a[:B], b[:B]], axis=0).astype(BF16)
        T[16 * j:16 * j + 16, D // 2:] = jnp.concatenate([a[B:], b[B:]], axis=0).astype(BF16)

    mine = pl.ds(pl.multiple_of(n * R2, R2), R2)

    def partial(c):
        at = pl.ds(chunks[c][0], chunks[c][1])
        return remote(xsend.at[:, :, at], xrecv.at[:, :, at], p_s.at[c], p_r.at[c], narrow=1 - n)

    def spread(c):
        at = pl.ds(chunks[c][0], chunks[c][1])
        return remote(hid.at[mine, at], hid.at[mine, at], h_s.at[c], h_r.at[c], narrow=1 - n)

    def widen(c):
        o, k = chunks[c]
        at = slice(o, o + k)
        for i, (wait, ref) in enumerate(((gates[c], wg), (ups[c], wu))):
            wait.wait()
            r = jnp.dot(T[...], ref[:, at], preferred_element_type=F32)
            first = n == 0
            own[i, :, at] = jnp.where(first, r[:R2], r[R2:])
            xsend[i, :, at] = jnp.where(first, r[R2:], r[:R2]).astype(BF16)
        go(partial(c))

    def activate(c):
        o, k = chunks[c]
        at = slice(o, o + k)
        partial(c).wait_recv()
        a = own[0, :, at] + xrecv[0, :, at].astype(F32)
        b = own[1, :, at] + xrecv[1, :, at].astype(F32)
        hid[mine, at] = (a / (1.0 + jnp.exp(-a)) * b).astype(BF16)
        go(spread(c))

    def narrow_down(i, after=None):
        group = down_groups[i]
        for c in group:
            downs[c].wait()
            spread(c).wait_recv()
        lo, hi = chunks[group[0]][0], chunks[group[-1]][0] + chunks[group[-1]][1]
        for t, (o, k) in enumerate(tiles):
            r = jnp.dot(hid[:, lo:hi], wd[lo:hi, o:o + k], preferred_element_type=F32)
            if i > 0:
                r = r + acc[:, o:o + k]
            acc[:, o:o + k] = r
            if after is not None:
                after(t)

    lag = 2
    C = len(chunks)
    ready = {grp[-1]: i for i, grp in enumerate(down_groups)}
    last = len(down_groups) - 1

    def core_sum(t):
        at = pl.ds(*tiles[t])
        theirs = pl.ds(pl.multiple_of((1 - s) * R2, R2), R2)
        return remote(acc.at[theirs, at], srecv.at[:, at], s_s.at[t], s_r.at[t], sub=1 - s)

    def y_sum(t):
        at = pl.ds(*tiles[t])
        return remote(ysend.at[:, at], yrecv.at[:, at], y_s.at[t], y_r.at[t], groups=1 - g)

    for c in range(C + lag + 2):
        if c < C:
            widen(c)
        if 0 <= c - lag < C:
            activate(c - lag)
        i = ready.get(c - lag - 2)
        if i is not None:
            narrow_down(i, (lambda t: go(core_sum(t))) if i == last else None)

    def rows(base):
        return pl.ds(pl.multiple_of(base, R4), R4)

    for t, (o, k) in enumerate(tiles):
        core_sum(t).wait_recv()
        at = slice(o, o + k)
        ysend[:, at] = (acc[rows(s * R2 + (1 - g) * R4), at] + srecv[rows((1 - g) * R4), at]).astype(BF16)
        go(y_sum(t))

    def z_send(t, o):
        return remote(zsend.at[t, o], zrecv.at[t, w], z_s.at[t, o], z_r.at[t, w], wide=o)

    def z_arrival(t, o):
        return remote(zsend.at[t, o], zrecv.at[t, o], z_s.at[t, o], z_r.at[t, o], wide=o)

    for t, (o, k) in enumerate(tiles):
        y_sum(t).wait_recv()
        at = slice(o, o + k)
        r = acc[rows(s * R2 + g * R4), at] + srecv[rows(g * R4), at] + yrecv[:, at].astype(F32)
        oacc[:, at] = r
        for ww in range(W):
            v = r[ww * B:(ww + 1) * B]
            zsend[t, ww] = jnp.concatenate([v[:, : k // 2], v[:, k // 2:]], axis=0).astype(BF16)
        for p in others:
            go(z_send(t, p))

    for t, (o, k) in enumerate(tiles):
        r = oacc[pl.ds(pl.multiple_of(w * B, B), B), o:o + k]
        for p in others:
            z_arrival(t, p).wait_recv()
            v = zrecv[t, p].astype(F32)
            r = r + jnp.concatenate([v[:B], v[B:]], axis=1)
        out_ref[:, o:o + k] = r.astype(BF16)

    for copy in sends:
        copy.wait_send()


def fused(W, tokens, gate_weight, up_weight, down_weight):
    B, D = tokens.shape
    H = gate_weight.shape[1]
    HU = H // 2
    N = down_weight.shape[1]
    R = 4 * W * B
    chunks = chunks_of(HU, 256)
    C = len(chunks)
    down_groups = [tuple(range(i, min(i + 2, C))) for i in range(0, C, 2)]
    tiles = chunks_of(N, 1024)
    NT = len(tiles)
    dma = pltpu.SemaphoreType.DMA
    scratch = [
        pltpu.VMEM((D, HU), BF16), pltpu.VMEM((D, HU), BF16), pltpu.VMEM((HU, N), BF16),
        pltpu.VMEM((4 * W, 2 * B, D // 2), BF16), pltpu.VMEM((R, D), BF16),
        pltpu.VMEM((2, R // 2, HU), F32), pltpu.VMEM((2, R // 2, HU), BF16), pltpu.VMEM((2, R // 2, HU), BF16),
        pltpu.VMEM((R, HU), BF16), pltpu.VMEM((R, N), F32), pltpu.VMEM((R // 2, N), F32),
        pltpu.VMEM((R // 4, N), BF16), pltpu.VMEM((R // 4, N), BF16), pltpu.VMEM((R // 4, N), F32),
        pltpu.VMEM((NT, W, 2 * B, tiles[0][1] // 2), BF16), pltpu.VMEM((NT, W, 2 * B, tiles[0][1] // 2), BF16),
        dma((C,)), dma((C,)), dma((C,)),
        dma((W,)), dma((W,)), dma((2 * W,)), dma((4 * W,)),
        dma((C,)), dma((C,)), dma((C,)), dma((C,)),
        dma((NT,)), dma((NT,)), dma((NT,)), dma((NT,)), dma((NT, W)), dma((NT, W)),
    ]
    vmem, hbm = pl.BlockSpec(memory_space=pltpu.VMEM), pl.BlockSpec(memory_space=pl.ANY)
    return pl.pallas_call(
        functools.partial(kernel, W, chunks, down_groups, tiles),
        out_shape=jax.ShapeDtypeStruct((B, N), BF16),
        in_specs=[vmem, hbm, hbm, hbm],
        out_specs=vmem,
        scratch_shapes=scratch,
        compiler_params=pltpu.CompilerParams(
            collective_id=0, has_side_effects=True, vmem_limit_bytes=60 * 2**20),
        cost_estimate=pl.CostEstimate(
            flops=6 * R * D * HU, bytes_accessed=6 * D * HU, transcendentals=R * HU // 2),
    )(tokens, gate_weight, up_weight, down_weight)


def fits(mesh, tokens, gate_weight, down_weight):
    size = mesh.shape
    rows, hidden, columns = tokens.shape[0], gate_weight.shape[1], down_weight.shape[1]
    return (
        size["groups"] == 2 and size["narrow"] == 2 and size["sub"] == 2 and size["wide"] <= 4
        and rows == 8 and hidden % 256 == 0 and columns % 1024 == 0
        and 3 * tokens.shape[1] * hidden <= 48 * 2**20
    )


def solution(mesh):
    def per_device(tokens, gate_weight, up_weight, down_weight):
        if fits(mesh, tokens, gate_weight, down_weight):
            return fused(mesh.shape["wide"], tokens, gate_weight, up_weight, down_weight)
        return plain(tokens, gate_weight, up_weight, down_weight)

    return jax.shard_map(
        per_device,
        mesh=mesh,
        in_specs=(
            P(("groups", "wide", "sub"), "narrow"),
            P("narrow", ("wide", "sub")),
            P("narrow", ("wide", "sub")),
            P(("wide", "sub"), "narrow"),
        ),
        out_specs=P(("groups", "wide", "sub"), "narrow"),
        check_vma=False,
    )
```

```python
import functools

import jax
import jax.numpy as jnp
from jax import lax
from jax.experimental import pallas as pl
from jax.experimental.pallas import tpu as pltpu
from jax.sharding import PartitionSpec as P

MESH = pl.DeviceIdType.MESH
F32 = jnp.float32
BF16 = jnp.bfloat16


def plain(tokens, gate_weight, up_weight, down_weight):
    segment = lax.all_gather(tokens, ("wide", "sub"), axis=0, tiled=True)
    gate_part = jnp.dot(segment, gate_weight, preferred_element_type=F32)
    up_part = jnp.dot(segment, up_weight, preferred_element_type=F32)
    totals = lax.psum(jnp.stack([gate_part, up_part]), "narrow")
    hidden = (jax.nn.silu(totals[0]) * totals[1]).astype(BF16)
    output_block = lax.psum_scatter(
        jnp.dot(hidden, down_weight, preferred_element_type=F32),
        ("wide", "sub"),
        scatter_dimension=0,
        tiled=True,
    )
    return output_block.astype(BF16)


def chunks_of(extent, width):
    return [(o, min(width, extent - o)) for o in range(0, extent, width)]


def kernel(W, chunks, down_groups, tiles,
           x_ref, gate_ref, up_ref, down_ref, out_ref,
           wg, wu, wd, tok, T, own, xsend, xrecv, hid, acc, srecv, ysend, yrecv, oacc, zsend, zrecv,
           wg_sem, wu_sem, wd_sem, tz_s, ty_s, tc_s, t_r, p_s, p_r, h_s, h_r,
           s_s, s_r, y_s, y_r, z_s, z_r):
    g, w, n, s = (lax.axis_index(a) for a in ("groups", "wide", "narrow", "sub"))
    B, D = x_ref.shape
    HU = wg.shape[1]
    R = T.shape[0]
    R2, R4 = R // 2, R // 4

    def weight_copy(src, dst, sems, c, rows):
        o, k = chunks[c]
        at = pl.ds(pl.multiple_of(g * HU + o, 128), k)
        if rows:
            return pltpu.make_async_copy(src.at[at, :], dst.at[pl.ds(o, k), :], sems.at[c])
        return pltpu.make_async_copy(src.at[:, at], dst.at[:, pl.ds(o, k)], sems.at[c])

    gates = [weight_copy(gate_ref, wg, wg_sem, c, False) for c in range(len(chunks))]
    ups = [weight_copy(up_ref, wu, wu_sem, c, False) for c in range(len(chunks))]
    downs = [weight_copy(down_ref, wd, wd_sem, c, True) for c in range(len(chunks))]
    for c in range(len(chunks)):
        gates[c].start()
        ups[c].start()
    for d in downs:
        d.start()

    def remote(src, dst, send, recv, **to):
        return pltpu.make_async_remote_copy(
            src_ref=src, dst_ref=dst, send_sem=send, recv_sem=recv, device_id=to, device_id_type=MESH)

    others = [lax.rem(w + d, W) for d in range(1, W)]
    barrier = pltpu.get_barrier_semaphore()
    for to in [{"wide": o} for o in others] + [{"groups": 1 - g}, {"sub": 1 - s}, {"narrow": 1 - n}]:
        pl.semaphore_signal(barrier, inc=1, device_id=to, device_id_type=MESH)
    x = x_ref[...].astype(F32)
    block = lambda gg, ww, ss: ss * (2 * W) + gg * W + ww
    me = block(g, w, s)
    tok[me] = jnp.concatenate([x[:, : D // 2], x[:, D // 2:]], axis=0).astype(BF16)
    pl.semaphore_wait(barrier, W + 2)

    sends = []

    def go(copy):
        copy.start()
        sends.append(copy)

    def to_z(b, o):
        return remote(tok.at[b], tok.at[b], tz_s.at[o], t_r.at[b], wide=o)

    def to_y(b, o):
        return remote(tok.at[b], tok.at[b], ty_s.at[o], t_r.at[b], groups=1 - g)

    def to_core(b, i):
        return remote(tok.at[b], tok.at[b], tc_s.at[i], t_r.at[b], sub=1 - s)

    for o in others:
        go(to_z(me, o))
    go(to_y(me, w))
    go(to_core(me, g * W + w))
    for o in others:
        b = block(g, o, s)
        to_z(b, o).wait_recv()
        go(to_y(b, o))
        go(to_core(b, g * W + o))
    for o in [w] + others:
        b = block(1 - g, o, s)
        to_y(b, o).wait_recv()
        go(to_core(b, (1 - g) * W + o))
    for gg in range(2):
        for ww in range(W):
            to_core(block(gg, ww, 1 - s), gg * W + ww).wait_recv()

    for j in range(R // 16):
        a = tok[2 * j].astype(F32)
        b = tok[2 * j + 1].astype(F32)
        T[16 * j:16 * j + 16, : D // 2] = jnp.concatenate([a[:B], b[:B]], axis=0).astype(BF16)
        T[16 * j:16 * j + 16, D // 2:] = jnp.concatenate([a[B:], b[B:]], axis=0).astype(BF16)

    def mine(h):
        return pl.ds(pl.multiple_of(h * R2 + n * R4, R4), R4)

    C = len(chunks)

    def partial(h, c):
        at = pl.ds(chunks[c][0], chunks[c][1])
        return remote(xsend.at[h, :, :, at], xrecv.at[h, :, :, at], p_s.at[h, c], p_r.at[h, c], narrow=1 - n)

    def spread(h, c):
        at = pl.ds(chunks[c][0], chunks[c][1])
        return remote(hid.at[mine(h), at], hid.at[mine(h), at], h_s.at[h, c], h_r.at[h, c], narrow=1 - n)

    def widen(h, c):
        o, k = chunks[c]
        at = slice(o, o + k)
        if h == 0:
            gates[c].wait()
            ups[c].wait()
        first = n == 0
        for i, ref in enumerate((wg, wu)):
            r = jnp.dot(T[h * R2:(h + 1) * R2, :], ref[:, at], preferred_element_type=F32)
            own[h, i, :, at] = jnp.where(first, r[:R4], r[R4:])
            xsend[h, i, :, at] = jnp.where(first, r[R4:], r[:R4]).astype(BF16)
        go(partial(h, c))

    def activate(h, c):
        o, k = chunks[c]
        at = slice(o, o + k)
        partial(h, c).wait_recv()
        a = own[h, 0, :, at] + xrecv[h, 0, :, at].astype(F32)
        b = own[h, 1, :, at] + xrecv[h, 1, :, at].astype(F32)
        hid[mine(h), at] = (a / (1.0 + jnp.exp(-a)) * b).astype(BF16)
        go(spread(h, c))

    def core_sum(t):
        at = pl.ds(*tiles[t])
        theirs = pl.ds(pl.multiple_of((1 - s) * R2, R2), R2)
        return remote(acc.at[theirs, at], srecv.at[:, at], s_s.at[t], s_r.at[t], sub=1 - s)

    def narrow_down(h, i):
        group = down_groups[i]
        for c in group:
            if h == 0:
                downs[c].wait()
            spread(h, c).wait_recv()
        lo, hi = chunks[group[0]][0], chunks[group[-1]][0] + chunks[group[-1]][1]
        half = slice(h * R2, (h + 1) * R2)
        for t, (base, k) in enumerate(tiles):
            for o in range(base, base + k, 1024):
                r = jnp.dot(hid[half, lo:hi], wd[lo:hi, o:o + 1024], preferred_element_type=F32)
                if i > 0:
                    r = r + acc[half, o:o + 1024]
                acc[half, o:o + 1024] = r
            if i == len(down_groups) - 1:
                @pl.when(s != h)
                def _():
                    core_sum(t).start()

    def rows(base):
        return pl.ds(pl.multiple_of(base, R4), R4)

    def y_sum(t):
        at = pl.ds(*tiles[t])
        return remote(ysend.at[:, at], yrecv.at[:, at], y_s.at[t], y_r.at[t], groups=1 - g)

    def z_send(t, o):
        return remote(zsend.at[t, o], zrecv.at[t, w], z_s.at[t, o], z_r.at[t, w], wide=o)

    def z_arrival(t, o):
        return remote(zsend.at[t, o], zrecv.at[t, o], z_s.at[t, o], z_r.at[t, o], wide=o)

    def over_y(h):
        for t, (o, k) in enumerate(tiles):
            core_sum(t).wait_recv()
            at = slice(o, o + k)
            ysend[:, at] = (acc[rows(h * R2 + (1 - g) * R4), at] + srecv[rows((1 - g) * R4), at]).astype(BF16)
            y_sum(t).start()

    def over_z(h):
        for t, (o, k) in enumerate(tiles):
            y_sum(t).wait_recv()
            at = slice(o, o + k)
            r = acc[rows(h * R2 + g * R4), at] + srecv[rows(g * R4), at] + yrecv[:, at].astype(F32)
            oacc[:, at] = r
            for ww in range(W):
                v = r[ww * B:(ww + 1) * B]
                zsend[t, ww] = jnp.concatenate([v[:, : k // 2], v[:, k // 2:]], axis=0).astype(BF16)
            for d in range(1, W):
                z_send(t, lax.rem(w + d, W)).start()

    steps = [(h, c) for h in range(2) for c in range(C)]
    ready = {grp[-1]: i for i, grp in enumerate(down_groups)}
    lag = 2
    for q in range(len(steps) + 2 * lag):
        if q < len(steps):
            widen(*steps[q])
        if 0 <= q - lag < len(steps):
            activate(*steps[q - lag])
        if 0 <= q - 2 * lag < len(steps):
            h, c = steps[q - 2 * lag]
            if c in ready:
                narrow_down(h, ready[c])
            if (h, c) == (1, 0):
                pl.when(s == 0)(lambda: over_y(0))
            if (h, c) == (1, C - 2):
                pl.when(s == 0)(lambda: over_z(0))

    @pl.when(s == 1)
    def _():
        over_y(1)
        over_z(1)

    for t, (o, k) in enumerate(tiles):
        r = oacc[pl.ds(pl.multiple_of(w * B, B), B), o:o + k]
        for p in others:
            z_arrival(t, p).wait_recv()
            v = zrecv[t, p].astype(F32)
            r = r + jnp.concatenate([v[:B], v[B:]], axis=1)
        out_ref[:, o:o + k] = r.astype(BF16)

    for copy in sends:
        copy.wait_send()
    for t in range(len(tiles)):
        core_sum(t).wait_send()
        y_sum(t).wait_send()
        for p in others:
            z_send(t, p).wait_send()


def fused(W, tokens, gate_weight, up_weight, down_weight):
    B, D = tokens.shape
    H = gate_weight.shape[1]
    HU = H // 2
    N = down_weight.shape[1]
    R = 4 * W * B
    chunks = chunks_of(HU, 512)
    C = len(chunks)
    down_groups = [(0, 1)] + [(c,) for c in range(2, C)]
    tiles = chunks_of(N, 2048)
    NT = len(tiles)
    dma = pltpu.SemaphoreType.DMA
    scratch = [
        pltpu.VMEM((D, HU), BF16), pltpu.VMEM((D, HU), BF16), pltpu.VMEM((HU, N), BF16),
        pltpu.VMEM((4 * W, 2 * B, D // 2), BF16), pltpu.VMEM((R, D), BF16),
        pltpu.VMEM((2, 2, R // 4, HU), F32), pltpu.VMEM((2, 2, R // 4, HU), BF16), pltpu.VMEM((2, 2, R // 4, HU), BF16),
        pltpu.VMEM((R, HU), BF16), pltpu.VMEM((R, N), F32), pltpu.VMEM((R // 2, N), F32),
        pltpu.VMEM((R // 4, N), BF16), pltpu.VMEM((R // 4, N), BF16), pltpu.VMEM((R // 4, N), F32),
        pltpu.VMEM((NT, W, 2 * B, tiles[0][1] // 2), BF16), pltpu.VMEM((NT, W, 2 * B, tiles[0][1] // 2), BF16),
        dma((C,)), dma((C,)), dma((C,)),
        dma((W,)), dma((W,)), dma((2 * W,)), dma((4 * W,)),
        dma((2, C)), dma((2, C)), dma((2, C)), dma((2, C)),
        dma((NT,)), dma((NT,)), dma((NT,)), dma((NT,)), dma((NT, W)), dma((NT, W)),
    ]
    vmem, hbm = pl.BlockSpec(memory_space=pltpu.VMEM), pl.BlockSpec(memory_space=pl.ANY)
    return pl.pallas_call(
        functools.partial(kernel, W, chunks, down_groups, tiles),
        out_shape=jax.ShapeDtypeStruct((B, N), BF16),
        in_specs=[vmem, hbm, hbm, hbm],
        out_specs=vmem,
        scratch_shapes=scratch,
        compiler_params=pltpu.CompilerParams(
            collective_id=0, has_side_effects=True, vmem_limit_bytes=60 * 2**20),
        cost_estimate=pl.CostEstimate(
            flops=6 * R * D * HU, bytes_accessed=6 * D * HU, transcendentals=R * HU // 2),
    )(tokens, gate_weight, up_weight, down_weight)


def fits(mesh, tokens, gate_weight, down_weight):
    size = mesh.shape
    rows, hidden, columns = tokens.shape[0], gate_weight.shape[1], down_weight.shape[1]
    return (
        size["groups"] == 2 and size["narrow"] == 2 and size["sub"] == 2 and size["wide"] <= 4
        and rows == 8 and size["wide"] % 4 == 0 and hidden % 256 == 0 and hidden >= 2048 and columns % 2048 == 0
        and 3 * tokens.shape[1] * hidden <= 48 * 2**20
    )


def solution(mesh):
    def per_device(tokens, gate_weight, up_weight, down_weight):
        if fits(mesh, tokens, gate_weight, down_weight):
            return fused(mesh.shape["wide"], tokens, gate_weight, up_weight, down_weight)
        return plain(tokens, gate_weight, up_weight, down_weight)

    return jax.shard_map(
        per_device,
        mesh=mesh,
        in_specs=(
            P(("groups", "wide", "sub"), "narrow"),
            P("narrow", ("wide", "sub")),
            P("narrow", ("wide", "sub")),
            P(("wide", "sub"), "narrow"),
        ),
        out_specs=P(("groups", "wide", "sub"), "narrow"),
        check_vma=False,
    )
```

```python
import functools

import jax
import jax.numpy as jnp
from jax import lax
from jax.experimental import pallas as pl
from jax.experimental.pallas import tpu as pltpu
from jax.sharding import PartitionSpec as P

MESH = pl.DeviceIdType.MESH
F32 = jnp.float32
BF16 = jnp.bfloat16


def plain(tokens, gate_weight, up_weight, down_weight):
    segment = lax.all_gather(tokens, ("wide", "sub"), axis=0, tiled=True)
    gate_part = jnp.dot(segment, gate_weight, preferred_element_type=F32)
    up_part = jnp.dot(segment, up_weight, preferred_element_type=F32)
    totals = lax.psum(jnp.stack([gate_part, up_part]), "narrow")
    hidden = (jax.nn.silu(totals[0]) * totals[1]).astype(BF16)
    output_block = lax.psum_scatter(
        jnp.dot(hidden, down_weight, preferred_element_type=F32),
        ("wide", "sub"),
        scatter_dimension=0,
        tiled=True,
    )
    return output_block.astype(BF16)


def chunks_of(extent, width):
    return [(o, min(width, extent - o)) for o in range(0, extent, width)]


def kernel(W, chunks, down_groups, tiles,
           x_ref, gate_ref, up_ref, down_ref, out_ref,
           wg, wu, wd, tok, T, own, xsend, xrecv, hid, acc, srecv, ysend, yrecv, oacc, zsend, zrecv,
           wg_sem, wu_sem, wd_sem, tz_s, ty_s, tc_s, t_r, p_s, p_r, h_s, h_r,
           s_s, s_r, y_s, y_r, z_s, z_r):
    g, w, n, s = (lax.axis_index(a) for a in ("groups", "wide", "narrow", "sub"))
    B, D = x_ref.shape
    HU = wg.shape[1]
    R = T.shape[0]
    R2, R4 = R // 2, R // 4

    others = [lax.rem(w + d, W) for d in range(1, W)]
    barrier = pltpu.get_barrier_semaphore()
    for to in [{"wide": o} for o in others] + [{"groups": 1 - g}, {"sub": 1 - s}, {"narrow": 1 - n}]:
        pl.semaphore_signal(barrier, inc=1, device_id=to, device_id_type=MESH)

    def weight_copy(src, dst, sems, c, rows):
        o, k = chunks[c]
        at = pl.ds(pl.multiple_of(g * HU + o, 128), k)
        if rows:
            return pltpu.make_async_copy(src.at[at, :], dst.at[pl.ds(o, k), :], sems.at[c])
        return pltpu.make_async_copy(src.at[:, at], dst.at[:, pl.ds(o, k)], sems.at[c])

    gates = [weight_copy(gate_ref, wg, wg_sem, c, False) for c in range(len(chunks))]
    ups = [weight_copy(up_ref, wu, wu_sem, c, False) for c in range(len(chunks))]
    downs = [weight_copy(down_ref, wd, wd_sem, c, True) for c in range(len(chunks))]
    for c in range(len(chunks)):
        gates[c].start()
        ups[c].start()
    for d in downs:
        d.start()

    def remote(src, dst, send, recv, **to):
        return pltpu.make_async_remote_copy(
            src_ref=src, dst_ref=dst, send_sem=send, recv_sem=recv, device_id=to, device_id_type=MESH)

    x = x_ref[...].astype(F32)
    block = lambda gg, ww, ss: ss * (2 * W) + gg * W + ww
    me = block(g, w, s)
    tok[me] = jnp.concatenate([x[:, : D // 2], x[:, D // 2:]], axis=0).astype(BF16)
    pl.semaphore_wait(barrier, W + 2)

    sends = []

    def go(copy):
        copy.start()
        sends.append(copy)

    def to_z(b, o):
        return remote(tok.at[b], tok.at[b], tz_s.at[o], t_r.at[b], wide=o)

    def to_y(b, o):
        return remote(tok.at[b], tok.at[b], ty_s.at[o], t_r.at[b], groups=1 - g)

    def to_core(b, i):
        return remote(tok.at[b], tok.at[b], tc_s.at[i], t_r.at[b], sub=1 - s)

    for o in others:
        go(to_z(me, o))
    go(to_y(me, w))
    go(to_core(me, g * W + w))
    for o in others:
        b = block(g, o, s)
        to_z(b, o).wait_recv()
        go(to_y(b, o))
        go(to_core(b, g * W + o))
    for o in [w] + others:
        b = block(1 - g, o, s)
        to_y(b, o).wait_recv()
        go(to_core(b, (1 - g) * W + o))
    for gg in range(2):
        for ww in range(W):
            to_core(block(gg, ww, 1 - s), gg * W + ww).wait_recv()

    for j in range(R // 16):
        a = tok[2 * j].astype(F32)
        b = tok[2 * j + 1].astype(F32)
        T[16 * j:16 * j + 16, : D // 2] = jnp.concatenate([a[:B], b[:B]], axis=0).astype(BF16)
        T[16 * j:16 * j + 16, D // 2:] = jnp.concatenate([a[B:], b[B:]], axis=0).astype(BF16)

    mine = pl.ds(pl.multiple_of(n * R2, R2), R2)

    def partial(c):
        at = pl.ds(chunks[c][0], chunks[c][1])
        return remote(xsend.at[:, :, at], xrecv.at[:, :, at], p_s.at[c], p_r.at[c], narrow=1 - n)

    def spread(c):
        at = pl.ds(chunks[c][0], chunks[c][1])
        return remote(hid.at[mine, at], hid.at[mine, at], h_s.at[c], h_r.at[c], narrow=1 - n)

    def widen(c):
        o, k = chunks[c]
        at = slice(o, o + k)
        gates[c].wait()
        ups[c].wait()
        for i, ref in enumerate((wg, wu)):
            r = jnp.dot(T[...], ref[:, at], preferred_element_type=F32)
            first = n == 0
            own[i, :, at] = jnp.where(first, r[:R2], r[R2:])
            xsend[i, :, at] = jnp.where(first, r[R2:], r[:R2]).astype(BF16)
        go(partial(c))

    def activate(c):
        o, k = chunks[c]
        at = slice(o, o + k)
        partial(c).wait_recv()
        a = own[0, :, at] + xrecv[0, :, at].astype(F32)
        b = own[1, :, at] + xrecv[1, :, at].astype(F32)
        hid[mine, at] = (a / (1.0 + jnp.exp(-a)) * b).astype(BF16)
        go(spread(c))

    def narrow_down(i, after=None):
        group = down_groups[i]
        for c in group:
            downs[c].wait()
            spread(c).wait_recv()
        lo, hi = chunks[group[0]][0], chunks[group[-1]][0] + chunks[group[-1]][1]
        for t, (o, k) in enumerate(tiles):
            r = jnp.dot(hid[:, lo:hi], wd[lo:hi, o:o + k], preferred_element_type=F32)
            if i > 0:
                r = r + acc[:, o:o + k]
            acc[:, o:o + k] = r
            if after is not None:
                after(t)

    lag = 2
    C = len(chunks)
    ready = {grp[-1]: i for i, grp in enumerate(down_groups)}
    last = len(down_groups) - 1

    def core_sum(t):
        at = pl.ds(*tiles[t])
        theirs = pl.ds(pl.multiple_of((1 - s) * R2, R2), R2)
        return remote(acc.at[theirs, at], srecv.at[:, at], s_s.at[t], s_r.at[t], sub=1 - s)

    def y_sum(t):
        at = pl.ds(*tiles[t])
        return remote(ysend.at[:, at], yrecv.at[:, at], y_s.at[t], y_r.at[t], groups=1 - g)

    for c in range(C + lag + 2):
        if c < C:
            widen(c)
        if 0 <= c - lag < C:
            activate(c - lag)
        i = ready.get(c - lag - 2)
        if i is not None:
            narrow_down(i, (lambda t: go(core_sum(t))) if i == last else None)

    def rows(base):
        return pl.ds(pl.multiple_of(base, R4), R4)

    for t, (o, k) in enumerate(tiles):
        core_sum(t).wait_recv()
        at = slice(o, o + k)
        ysend[:, at] = (acc[rows(s * R2 + (1 - g) * R4), at] + srecv[rows((1 - g) * R4), at]).astype(BF16)
        go(y_sum(t))

    def z_send(t, o):
        return remote(zsend.at[t, o], zrecv.at[t, w], z_s.at[t, o], z_r.at[t, w], wide=o)

    def z_arrival(t, o):
        return remote(zsend.at[t, o], zrecv.at[t, o], z_s.at[t, o], z_r.at[t, o], wide=o)

    for t, (o, k) in enumerate(tiles):
        y_sum(t).wait_recv()
        at = slice(o, o + k)
        r = acc[rows(s * R2 + g * R4), at] + srecv[rows(g * R4), at] + yrecv[:, at].astype(F32)
        oacc[:, at] = r
        for ww in range(W):
            v = r[ww * B:(ww + 1) * B]
            zsend[t, ww] = jnp.concatenate([v[:, : k // 2], v[:, k // 2:]], axis=0).astype(BF16)
        for p in others:
            go(z_send(t, p))

    for t, (o, k) in enumerate(tiles):
        r = oacc[pl.ds(pl.multiple_of(w * B, B), B), o:o + k]
        for p in others:
            z_arrival(t, p).wait_recv()
            v = zrecv[t, p].astype(F32)
            r = r + jnp.concatenate([v[:B], v[B:]], axis=1)
        out_ref[:, o:o + k] = r.astype(BF16)

    for copy in sends:
        copy.wait_send()


def fused(W, tokens, gate_weight, up_weight, down_weight):
    B, D = tokens.shape
    H = gate_weight.shape[1]
    HU = H // 2
    N = down_weight.shape[1]
    R = 4 * W * B
    chunks = chunks_of(HU, 256)
    C = len(chunks)
    down_groups = [tuple(range(i, min(i + 2, C))) for i in range(0, C, 2)]
    tiles = chunks_of(N, 1024)
    NT = len(tiles)
    dma = pltpu.SemaphoreType.DMA
    scratch = [
        pltpu.VMEM((D, HU), BF16), pltpu.VMEM((D, HU), BF16), pltpu.VMEM((HU, N), BF16),
        pltpu.VMEM((4 * W, 2 * B, D // 2), BF16), pltpu.VMEM((R, D), BF16),
        pltpu.VMEM((2, R // 2, HU), F32), pltpu.VMEM((2, R // 2, HU), BF16), pltpu.VMEM((2, R // 2, HU), BF16),
        pltpu.VMEM((R, HU), BF16), pltpu.VMEM((R, N), F32), pltpu.VMEM((R // 2, N), F32),
        pltpu.VMEM((R // 4, N), BF16), pltpu.VMEM((R // 4, N), BF16), pltpu.VMEM((R // 4, N), F32),
        pltpu.VMEM((NT, W, 2 * B, tiles[0][1] // 2), BF16), pltpu.VMEM((NT, W, 2 * B, tiles[0][1] // 2), BF16),
        dma((C,)), dma((C,)), dma((C,)),
        dma((W,)), dma((W,)), dma((2 * W,)), dma((4 * W,)),
        dma((C,)), dma((C,)), dma((C,)), dma((C,)),
        dma((NT,)), dma((NT,)), dma((NT,)), dma((NT,)), dma((NT, W)), dma((NT, W)),
    ]
    vmem, hbm = pl.BlockSpec(memory_space=pltpu.VMEM), pl.BlockSpec(memory_space=pl.ANY)
    return pl.pallas_call(
        functools.partial(kernel, W, chunks, down_groups, tiles),
        out_shape=jax.ShapeDtypeStruct((B, N), BF16),
        in_specs=[vmem, hbm, hbm, hbm],
        out_specs=vmem,
        scratch_shapes=scratch,
        compiler_params=pltpu.CompilerParams(
            collective_id=0, has_side_effects=True, vmem_limit_bytes=60 * 2**20),
        cost_estimate=pl.CostEstimate(
            flops=6 * R * D * HU, bytes_accessed=6 * D * HU, transcendentals=R * HU // 2),
    )(tokens, gate_weight, up_weight, down_weight)


def fits(mesh, tokens, gate_weight, down_weight):
    size = mesh.shape
    rows, hidden, columns = tokens.shape[0], gate_weight.shape[1], down_weight.shape[1]
    return (
        size["groups"] == 2 and size["narrow"] == 2 and size["sub"] == 2 and size["wide"] <= 4
        and rows == 8 and hidden % 256 == 0 and columns % 1024 == 0
        and 3 * tokens.shape[1] * hidden <= 48 * 2**20
    )


def solution(mesh):
    def per_device(tokens, gate_weight, up_weight, down_weight):
        if fits(mesh, tokens, gate_weight, down_weight):
            return fused(mesh.shape["wide"], tokens, gate_weight, up_weight, down_weight)
        return plain(tokens, gate_weight, up_weight, down_weight)

    return jax.shard_map(
        per_device,
        mesh=mesh,
        in_specs=(
            P(("groups", "wide", "sub"), "narrow"),
            P("narrow", ("wide", "sub")),
            P("narrow", ("wide", "sub")),
            P(("wide", "sub"), "narrow"),
        ),
        out_specs=P(("groups", "wide", "sub"), "narrow"),
        check_vma=False,
    )
```

```python
import functools

import jax
import jax.numpy as jnp
from jax import lax
from jax.experimental import pallas as pl
from jax.experimental.pallas import tpu as pltpu
from jax.sharding import PartitionSpec as P

MESH = pl.DeviceIdType.MESH
F32 = jnp.float32
BF16 = jnp.bfloat16


def plain(tokens, gate_weight, up_weight, down_weight):
    segment = lax.all_gather(tokens, ("wide", "sub"), axis=0, tiled=True)
    gate_part = jnp.dot(segment, gate_weight, preferred_element_type=F32)
    up_part = jnp.dot(segment, up_weight, preferred_element_type=F32)
    totals = lax.psum(jnp.stack([gate_part, up_part]), "narrow")
    hidden = (jax.nn.silu(totals[0]) * totals[1]).astype(BF16)
    output_block = lax.psum_scatter(
        jnp.dot(hidden, down_weight, preferred_element_type=F32),
        ("wide", "sub"),
        scatter_dimension=0,
        tiled=True,
    )
    return output_block.astype(BF16)


def chunks_of(extent, width):
    return [(o, min(width, extent - o)) for o in range(0, extent, width)]


def kernel(W, chunks, down_groups, tiles,
           x_ref, gate_ref, up_ref, down_ref, out_ref,
           wg, wu, wd, tok, T, own, xsend, xrecv, hid, acc, srecv, ysend, yrecv, oacc, zsend, zrecv,
           wg_sem, wu_sem, wd_sem, tz_s, ty_s, tc_s, t_r, p_s, p_r, h_s, h_r,
           s_s, s_r, y_s, y_r, z_s, z_r):
    g, w, n, s = (lax.axis_index(a) for a in ("groups", "wide", "narrow", "sub"))
    B, D = x_ref.shape
    HU = wg.shape[1]
    R = T.shape[0]
    R2, R4 = R // 2, R // 4

    others = [lax.rem(w + d, W) for d in range(1, W)]
    barrier = pltpu.get_barrier_semaphore()
    for to in [{"wide": o} for o in others] + [{"groups": 1 - g}, {"sub": 1 - s}, {"narrow": 1 - n}]:
        pl.semaphore_signal(barrier, inc=1, device_id=to, device_id_type=MESH)

    def weight_copy(src, dst, sems, c, rows):
        o, k = chunks[c]
        at = pl.ds(pl.multiple_of(g * HU + o, 128), k)
        if rows:
            return pltpu.make_async_copy(src.at[at, :], dst.at[pl.ds(o, k), :], sems.at[c])
        return pltpu.make_async_copy(src.at[:, at], dst.at[:, pl.ds(o, k)], sems.at[c])

    gates = [weight_copy(gate_ref, wg, wg_sem, c, False) for c in range(len(chunks))]
    ups = [weight_copy(up_ref, wu, wu_sem, c, False) for c in range(len(chunks))]
    downs = [weight_copy(down_ref, wd, wd_sem, c, True) for c in range(len(chunks))]
    for c in range(len(chunks)):
        gates[c].start()
        ups[c].start()
    for d in downs:
        d.start()

    def remote(src, dst, send, recv, **to):
        return pltpu.make_async_remote_copy(
            src_ref=src, dst_ref=dst, send_sem=send, recv_sem=recv, device_id=to, device_id_type=MESH)

    x = x_ref[...].astype(F32)
    block = lambda gg, ww, ss: ss * (2 * W) + gg * W + ww
    me = block(g, w, s)
    tok[me] = jnp.concatenate([x[:, : D // 2], x[:, D // 2:]], axis=0).astype(BF16)
    pl.semaphore_wait(barrier, W + 2)

    sends = []

    def go(copy):
        copy.start()
        sends.append(copy)

    def to_z(b, o):
        return remote(tok.at[b], tok.at[b], tz_s.at[o], t_r.at[b], wide=o)

    def to_y(b, o):
        return remote(tok.at[b], tok.at[b], ty_s.at[o], t_r.at[b], groups=1 - g)

    def to_core(b, i):
        return remote(tok.at[b], tok.at[b], tc_s.at[i], t_r.at[b], sub=1 - s)

    for o in others:
        go(to_z(me, o))
    go(to_y(me, w))
    go(to_core(me, g * W + w))
    for o in others:
        b = block(g, o, s)
        to_z(b, o).wait_recv()
        go(to_y(b, o))
        go(to_core(b, g * W + o))
    for o in [w] + others:
        b = block(1 - g, o, s)
        to_y(b, o).wait_recv()
        go(to_core(b, (1 - g) * W + o))
    for gg in range(2):
        for ww in range(W):
            to_core(block(gg, ww, 1 - s), gg * W + ww).wait_recv()

    for j in range(R // 16):
        a = tok[2 * j].astype(F32)
        b = tok[2 * j + 1].astype(F32)
        T[16 * j:16 * j + 16, : D // 2] = jnp.concatenate([a[:B], b[:B]], axis=0).astype(BF16)
        T[16 * j:16 * j + 16, D // 2:] = jnp.concatenate([a[B:], b[B:]], axis=0).astype(BF16)

    mine = pl.ds(pl.multiple_of(n * R2, R2), R2)

    def partial(c):
        at = pl.ds(chunks[c][0], chunks[c][1])
        return remote(xsend.at[:, :, at], xrecv.at[:, :, at], p_s.at[c], p_r.at[c], narrow=1 - n)

    def spread(c):
        at = pl.ds(chunks[c][0], chunks[c][1])
        return remote(hid.at[mine, at], hid.at[mine, at], h_s.at[c], h_r.at[c], narrow=1 - n)

    def widen(c):
        o, k = chunks[c]
        at = slice(o, o + k)
        gates[c].wait()
        ups[c].wait()
        for i, ref in enumerate((wg, wu)):
            r = jnp.dot(T[...], ref[:, at], preferred_element_type=F32)
            first = n == 0
            own[i, :, at] = jnp.where(first, r[:R2], r[R2:])
            xsend[i, :, at] = jnp.where(first, r[R2:], r[:R2]).astype(BF16)
        go(partial(c))

    def activate(c):
        o, k = chunks[c]
        at = slice(o, o + k)
        partial(c).wait_recv()
        a = own[0, :, at] + xrecv[0, :, at].astype(F32)
        b = own[1, :, at] + xrecv[1, :, at].astype(F32)
        hid[mine, at] = (a / (1.0 + jnp.exp(-a)) * b).astype(BF16)
        go(spread(c))

    def narrow_down(i, after=None):
        group = down_groups[i]
        for c in group:
            downs[c].wait()
            spread(c).wait_recv()
        lo, hi = chunks[group[0]][0], chunks[group[-1]][0] + chunks[group[-1]][1]
        for t, (o, k) in enumerate(tiles):
            r = jnp.dot(hid[:, lo:hi], wd[lo:hi, o:o + k], preferred_element_type=F32)
            if i > 0:
                r = r + acc[:, o:o + k]
            acc[:, o:o + k] = r
            if after is not None:
                after(t)

    lag = 3
    C = len(chunks)
    ready = {grp[-1]: i for i, grp in enumerate(down_groups)}
    last = len(down_groups) - 1

    def core_sum(t):
        at = pl.ds(*tiles[t])
        theirs = pl.ds(pl.multiple_of((1 - s) * R2, R2), R2)
        return remote(acc.at[theirs, at], srecv.at[:, at], s_s.at[t], s_r.at[t], sub=1 - s)

    def y_sum(t):
        at = pl.ds(*tiles[t])
        return remote(ysend.at[:, at], yrecv.at[:, at], y_s.at[t], y_r.at[t], groups=1 - g)

    for c in range(C + lag + 2):
        if c < C:
            widen(c)
        if 0 <= c - lag < C:
            activate(c - lag)
        i = ready.get(c - lag - 2)
        if i is not None:
            narrow_down(i, (lambda t: go(core_sum(t))) if i == last else None)

    def rows(base):
        return pl.ds(pl.multiple_of(base, R4), R4)

    for t, (o, k) in enumerate(tiles):
        core_sum(t).wait_recv()
        at = slice(o, o + k)
        ysend[:, at] = (acc[rows(s * R2 + (1 - g) * R4), at] + srecv[rows((1 - g) * R4), at]).astype(BF16)
        go(y_sum(t))

    def z_send(t, o):
        return remote(zsend.at[t, o], zrecv.at[t, w], z_s.at[t, o], z_r.at[t, w], wide=o)

    def z_arrival(t, o):
        return remote(zsend.at[t, o], zrecv.at[t, o], z_s.at[t, o], z_r.at[t, o], wide=o)

    for t, (o, k) in enumerate(tiles):
        y_sum(t).wait_recv()
        at = slice(o, o + k)
        r = acc[rows(s * R2 + g * R4), at] + srecv[rows(g * R4), at] + yrecv[:, at].astype(F32)
        oacc[:, at] = r
        for ww in range(W):
            v = r[ww * B:(ww + 1) * B]
            zsend[t, ww] = jnp.concatenate([v[:, : k // 2], v[:, k // 2:]], axis=0).astype(BF16)
        for p in others:
            go(z_send(t, p))

    for t, (o, k) in enumerate(tiles):
        r = oacc[pl.ds(pl.multiple_of(w * B, B), B), o:o + k]
        for p in others:
            z_arrival(t, p).wait_recv()
            v = zrecv[t, p].astype(F32)
            r = r + jnp.concatenate([v[:B], v[B:]], axis=1)
        out_ref[:, o:o + k] = r.astype(BF16)

    for copy in sends:
        copy.wait_send()


def fused(W, tokens, gate_weight, up_weight, down_weight):
    B, D = tokens.shape
    H = gate_weight.shape[1]
    HU = H // 2
    N = down_weight.shape[1]
    R = 4 * W * B
    chunks = chunks_of(HU, 256)
    C = len(chunks)
    down_groups = [tuple(range(i, min(i + 2, C))) for i in range(0, C, 2)]
    tiles = chunks_of(N, 1024)
    NT = len(tiles)
    dma = pltpu.SemaphoreType.DMA
    scratch = [
        pltpu.VMEM((D, HU), BF16), pltpu.VMEM((D, HU), BF16), pltpu.VMEM((HU, N), BF16),
        pltpu.VMEM((4 * W, 2 * B, D // 2), BF16), pltpu.VMEM((R, D), BF16),
        pltpu.VMEM((2, R // 2, HU), F32), pltpu.VMEM((2, R // 2, HU), BF16), pltpu.VMEM((2, R // 2, HU), BF16),
        pltpu.VMEM((R, HU), BF16), pltpu.VMEM((R, N), F32), pltpu.VMEM((R // 2, N), F32),
        pltpu.VMEM((R // 4, N), BF16), pltpu.VMEM((R // 4, N), BF16), pltpu.VMEM((R // 4, N), F32),
        pltpu.VMEM((NT, W, 2 * B, tiles[0][1] // 2), BF16), pltpu.VMEM((NT, W, 2 * B, tiles[0][1] // 2), BF16),
        dma((C,)), dma((C,)), dma((C,)),
        dma((W,)), dma((W,)), dma((2 * W,)), dma((4 * W,)),
        dma((C,)), dma((C,)), dma((C,)), dma((C,)),
        dma((NT,)), dma((NT,)), dma((NT,)), dma((NT,)), dma((NT, W)), dma((NT, W)),
    ]
    vmem, hbm = pl.BlockSpec(memory_space=pltpu.VMEM), pl.BlockSpec(memory_space=pl.ANY)
    return pl.pallas_call(
        functools.partial(kernel, W, chunks, down_groups, tiles),
        out_shape=jax.ShapeDtypeStruct((B, N), BF16),
        in_specs=[vmem, hbm, hbm, hbm],
        out_specs=vmem,
        scratch_shapes=scratch,
        compiler_params=pltpu.CompilerParams(
            collective_id=0, has_side_effects=True, vmem_limit_bytes=60 * 2**20),
        cost_estimate=pl.CostEstimate(
            flops=6 * R * D * HU, bytes_accessed=6 * D * HU, transcendentals=R * HU // 2),
    )(tokens, gate_weight, up_weight, down_weight)


def fits(mesh, tokens, gate_weight, down_weight):
    size = mesh.shape
    rows, hidden, columns = tokens.shape[0], gate_weight.shape[1], down_weight.shape[1]
    return (
        size["groups"] == 2 and size["narrow"] == 2 and size["sub"] == 2 and size["wide"] <= 4
        and rows == 8 and hidden % 256 == 0 and columns % 1024 == 0
        and 3 * tokens.shape[1] * hidden <= 48 * 2**20
    )


def solution(mesh):
    def per_device(tokens, gate_weight, up_weight, down_weight):
        if fits(mesh, tokens, gate_weight, down_weight):
            return fused(mesh.shape["wide"], tokens, gate_weight, up_weight, down_weight)
        return plain(tokens, gate_weight, up_weight, down_weight)

    return jax.shard_map(
        per_device,
        mesh=mesh,
        in_specs=(
            P(("groups", "wide", "sub"), "narrow"),
            P("narrow", ("wide", "sub")),
            P("narrow", ("wide", "sub")),
            P(("wide", "sub"), "narrow"),
        ),
        out_specs=P(("groups", "wide", "sub"), "narrow"),
        check_vma=False,
    )
```
